768 devices in a mesh: pts: 96 (over y, z), grp: 8 (over x, core).
Axes of the slice: x: 4, y: 8, z: 12, core: 2. Of those that a mesh axis runs over, the one named last changes fastest.
Arguments:
- points: bfloat16 [786432, 1024], P(('pts', 'grp')), may hold values from -24 to 24
- send_counts: int32 [768, 8], P(('pts', 'grp')), may hold values from 16 to 128, as said below
- assign_one: int32 [786432], P(('pts', 'grp')), may hold values from 0 to 127, as said below
- parent_two: int32 [98304], P(('pts', 'grp')), may hold values from 0 to 255, as said below
- parent_three: int32 [256], replicated, may hold values from 0 to 31, as said below
- parent_four: int32 [32], replicated, may hold values from 0 to 7, as said below
Outputs:
- centroids_one: float32 [98304, 1024], P(('pts', 'grp'))
- centroids_two: float32 [256, 1024], replicated
- centroids_three: float32 [32, 1024], replicated
- centroids_four: float32 [8, 1024], replicated
The draws below stay inside these ranges and needn't reach their ends.
Inputs may be any that keep to these rules, and one draw needn't show every extreme that they name: `send_counts`: blocks are filled from their first slot; for each pts index one block index, drawn from the seed, is full (128) on every device of that pts index. `assign_one`: every level-1 centroid is named by at least one live slot. `parent_two`: every level-2 centroid has at least one child. `parent_three`: every level-3 centroid has at least one child. `parent_four`: every level-4 centroid has at least one child.
All inputs are finite; a program needn't handle non-finite values.
Results may differ from the reference program's by a relative error of at most 0.0003.
Values may be sent and summed in bfloat16 or wider, within the bound.
No kernel may reach another device: no remote copies, remote signals or barrier semaphores. Data moves between devices by JAX's collectives and lax.ppermute only.
A program may use at most 32 MiB of HBM per device.

```python
import jax
import jax.numpy as jnp
from jax import lax

D = 1024
CAP = 128
K1_DEV = 128
K2 = 256
K3 = 32
K4 = 8
ROWS = 786432
K1 = 98304
N_PTS = 96
N_GRP = 8


def draw_send_counts(key, part):
    key = jax.random.fold_in(key, 11)
    ndevice = N_PTS * N_GRP
    least = K1_DEV // N_GRP
    first_key, second_key, third_key = jax.random.split(key, 3)
    first = jax.random.randint(first_key, (ndevice, N_GRP), least, CAP + 1)
    second = jax.random.randint(second_key, (ndevice, N_GRP), least, CAP + 1)
    base = jnp.minimum(first, second)
    full = jax.random.randint(third_key, (N_PTS,), 0, N_GRP)
    fullmask = jnp.arange(N_GRP, dtype=jnp.int32)[None, :] == jnp.repeat(full, N_GRP)[:, None]
    return jnp.where(fullmask, CAP, base).astype(jnp.int32)


def draw_assign_one(key, part):
    key = jax.random.fold_in(key, 12)
    total = N_PTS * N_GRP * N_GRP * CAP
    least = K1_DEV // N_GRP
    index = jnp.arange(total, dtype=jnp.int32)
    device = index // (N_GRP * CAP)
    within = index % CAP
    source = device % N_GRP
    random_ids = jax.random.randint(key, (total,), 0, K1_DEV)
    return jnp.where(within < least, source * least + within, random_ids).astype(jnp.int32)


def covering(key, length, count):
    index = jnp.arange(length, dtype=jnp.int32)
    random_ids = jax.random.randint(key, (length,), 0, count)
    return jnp.where(index < count, index, random_ids).astype(jnp.int32)


def draw_parent_two(key, part):
    key = jax.random.fold_in(key, 13)
    return covering(key, K1, K2)


def draw_parent_three(key, part):
    key = jax.random.fold_in(key, 14)
    return covering(key, K2, K3)


def draw_parent_four(key, part):
    key = jax.random.fold_in(key, 15)
    return covering(key, K3, K4)


def shard_levels(own_key, shape, cuts, low, top_value):
    loudness, own = 1.0, jax.random.fold_in(own_key, 6)
    for axis_at, parts in cuts:
        draws = jnp.exp(jax.random.uniform(jax.random.fold_in(own, axis_at), (parts,), jnp.float32, low / len(cuts), top_value / len(cuts)))
        loudness = loudness * jnp.repeat(draws, shape[axis_at] // parts).reshape([-1 if axis == axis_at else 1 for axis in range(len(shape))])
    return loudness


def centred(stream_key, shape, width, reach, shards=(), held_as=jnp.bfloat16):
    result = jax.random.normal(stream_key, shape, jnp.float32) * width
    if len(shards) > 0:
        result = shard_levels(stream_key, shape, shards, -0.22, 0.18) * result
    return jnp.clip(result, min=-reach, max=reach).astype(held_as)


def setup_inputs(seed: int = 0) -> dict:
    key_of = jax.random.split(jax.random.key(seed), 7)
    points = centred(key_of[0], (ROWS, D), 4.0, 24.0, ((0, 768),))
    send_counts = draw_send_counts(jax.random.fold_in(key_of[6], 71), 0)
    assign_one = draw_assign_one(jax.random.fold_in(key_of[6], 71), 0)
    parent_two = draw_parent_two(jax.random.fold_in(key_of[6], 71), 0)
    parent_three = draw_parent_three(jax.random.fold_in(key_of[6], 71), 0)
    parent_four = draw_parent_four(jax.random.fold_in(key_of[6], 71), 0)
    return {"points": points, "send_counts": send_counts, "assign_one": assign_one, "parent_two": parent_two, "parent_three": parent_three, "parent_four": parent_four}


def level_mean(rows, parents, count):
    sums = jax.ops.segment_sum(rows, parents, num_segments=count)
    numbers = jax.ops.segment_sum(jnp.ones(parents.shape, jnp.float32), parents, num_segments=count)
    return sums / numbers[:, None], numbers


def reference(points, send_counts, assign_one, parent_two, parent_three, parent_four):
    ndevice = N_PTS * N_GRP
    slots = N_GRP * CAP
    blocks = points.reshape(ndevice, slots, D)
    idents = assign_one.reshape(ndevice, slots)
    slot = jnp.arange(slots, dtype=jnp.int32)
    block = slot // CAP
    within = slot % CAP

    def step(carry, inputs):
        sums, numbers = carry
        rows, ids, counts, device = inputs
        weight = (within < counts[block]).astype(jnp.float32)
        target = ((device // N_GRP) * N_GRP + block) * K1_DEV + ids
        sums = sums.at[target].add(rows.astype(jnp.float32) * weight[:, None])
        numbers = numbers.at[target].add(weight)
        return (sums, numbers), None

    start = (jnp.zeros((K1, D), jnp.float32), jnp.zeros((K1,), jnp.float32))
    (sums_one, count_one), unused = lax.scan(step, start, (blocks, idents, send_counts, jnp.arange(ndevice, dtype=jnp.int32)))
    centroids_one = sums_one / count_one[:, None]
    centroids_two, unused_two = level_mean(centroids_one, parent_two, K2)
    centroids_three, unused_three = level_mean(centroids_two, parent_three, K3)
    centroids_four, unused_four = level_mean(centroids_three, parent_four, K4)
    return centroids_one, centroids_two, centroids_three, centroids_four
```

```python
import jax
import jax.numpy as jnp
from jax import lax
from jax.sharding import Mesh, PartitionSpec as P

K2 = 256
K3 = 32
K4 = 8
F32 = jnp.float32
BF16 = jnp.bfloat16


def dot(a, b, dims, precision=None):
    return lax.dot_general(a, b, (dims, ((), ())), precision=precision, preferred_element_type=F32)


def split_three(w):
    hi = lax.reduce_precision(w, 8, 7)
    rest = w - hi
    mid = lax.reduce_precision(rest, 8, 7)
    return hi, mid, rest - mid


def coarse_mean(rows, parents, count):
    onehot = (parents[None, :] == jnp.arange(count, dtype=jnp.int32)[:, None]).astype(F32)
    sums = dot(onehot, rows, ((1,), (0,)), lax.Precision.HIGHEST)
    return sums / jnp.sum(onehot, axis=1)[:, None]


def gather(rows, axes, n):
    wide = jnp.broadcast_to(rows[None], (n,) + rows.shape)
    return lax.all_to_all(wide, axes, split_axis=0, concat_axis=0, tiled=True)


def local(points, send_counts, assign_one, parent_two, parent_three, parent_four):
    nx, nc, npts = lax.axis_size("x"), lax.axis_size("c"), lax.axis_size("pts")
    groups = nx * nc
    slots, depth = points.shape
    cap = slots // groups
    kdev = parent_two.shape[0]
    half = depth // nc
    cols = half // nx
    x, c = lax.axis_index("x"), lax.axis_index("c")

    mine = lax.dynamic_slice_in_dim(points, c * half, half, 1)
    theirs = lax.ppermute(
        lax.dynamic_slice_in_dim(points, (1 - c) * half, half, 1), "c", [(0, 1), (1, 0)]
    )

    within = lax.broadcasted_iota(jnp.int32, (groups, cap), 1)
    idents = jnp.where(
        within < send_counts.reshape(groups, 1), assign_one.reshape(groups, cap), -1
    )
    pad = jnp.zeros((16 - groups - 1, cap), jnp.int32)
    known = gather(jnp.concatenate([idents, parent_two[None], pad]), ("x", "c"), groups)
    ids = known[:, :groups]
    parents = known[:, groups]

    ks = jnp.arange(kdev, dtype=jnp.int32)
    count_one = jnp.sum((ids[:, :, None, :] == ks[None, None, :, None]).astype(F32), axis=(0, 3))
    inverse = 1.0 / count_one
    child = jnp.sum(
        (parents.reshape(1, -1) == jnp.arange(K2, dtype=jnp.int32)[:, None]).astype(F32), axis=1
    )

    partial = 0.0
    for core, rows in ((c, mine), (1 - c, theirs)):
        own = lax.dynamic_index_in_dim(ids, x * nc + core, 0, keepdims=False)
        hit = own[:, None, :] == ks[None, :, None]
        weight = jnp.sum(jnp.where(hit, inverse[:, :, None], 0.0), axis=1).reshape(slots)
        key = jnp.sum(jnp.where(hit, parents[:, :, None] + 1, 0), axis=1).reshape(slots) - 1
        chosen = key[None, :] == jnp.arange(K2, dtype=jnp.int32)[:, None]
        for part in split_three(weight):
            onehot = jnp.where(chosen, part[None, :], 0.0).astype(BF16)
            partial = partial + dot(onehot, rows, ((1,), (0,)))
    partial = partial.reshape(K2, nx, cols).transpose(1, 0, 2)
    sums = jnp.sum(
        lax.all_to_all(partial, "x", split_axis=0, concat_axis=0, tiled=True), axis=0
    )
    r = -(-K2 // npts)
    extra = r * npts - K2
    sums = jnp.pad(sums, ((0, extra), (0, 0))).reshape(npts, r, cols)
    child = jnp.pad(jnp.pad(child, (0, extra)).reshape(npts, 1, r), ((0, 0), (0, 0), (0, cols - r)))
    both = lax.all_to_all(
        jnp.concatenate([sums, child], axis=1), "pts", split_axis=0, concat_axis=0, tiled=True
    )
    both = jnp.sum(both, axis=0)
    cent = both[:r] / both[r, :r][:, None]
    two = gather(cent, "pts", npts).reshape(npts * r, cols)[:K2]
    three = coarse_mean(two, parent_three, K3)
    four = coarse_mean(three, parent_four, K4)
    upper = gather(jnp.concatenate([two, three, four]), ("x", "c"), groups)
    upper = upper.reshape(nx, nc, K2 + K3 + K4, cols).transpose(2, 1, 0, 3)
    upper = upper.reshape(K2 + K3 + K4, depth)

    blocks = [v.reshape(nx, nc, cap, half) for v in (mine, theirs)]
    sums_one = [0.0] * nc
    for k in range(nx):
        to = lax.rem(x + k, nx)
        sent = jnp.stack([lax.dynamic_index_in_dim(v, to, 0, keepdims=False) for v in blocks])
        if k > 0:
            sent = lax.ppermute(sent, "x", [(j, (j + k) % nx) for j in range(nx)])
        source = lax.rem(x + nx - k, nx)
        for which, core in ((0, c), (1, 1 - c)):
            from_ids = lax.dynamic_index_in_dim(ids, source * nc + core, 0, keepdims=False)
            for o in range(nc):
                to_ids = lax.dynamic_index_in_dim(from_ids, x * nc + o, 0, keepdims=False)
                onehot = (to_ids[None, :] == ks[:, None]).astype(BF16)
                sums_one[o] = sums_one[o] + dot(onehot, sent[which, o], ((1,), (0,)))
    one = jnp.stack(sums_one) / lax.dynamic_slice_in_dim(count_one, x * nc, nc, 0)[:, :, None]
    kept = lax.dynamic_index_in_dim(one, c, 0, keepdims=False)
    given = lax.ppermute(
        lax.dynamic_index_in_dim(one, 1 - c, 0, keepdims=False), "c", [(0, 1), (1, 0)]
    )
    one = jnp.where(
        c == 0, jnp.concatenate([kept, given], 1), jnp.concatenate([given, kept], 1)
    )
    return one, upper[:K2], upper[K2 : K2 + K3], upper[K2 + K3 :]


def solution(mesh):
    npts, groups = mesh.devices.shape
    fine = Mesh(mesh.devices.reshape(npts, groups // 2, 2), ("pts", "x", "c"))
    every = ("pts", "x", "c")
    placed = (P(every, None), P(every, None), P(every), P(every), P(), P())
    return jax.shard_map(
        local,
        mesh=fine,
        in_specs=placed,
        out_specs=(P(every, None), P(), P(), P()),
        check_vma=False,
    )
```

```python
import jax
import jax.numpy as jnp
from jax import lax
from jax.experimental import pallas as pl
from jax.experimental.pallas import tpu as pltpu
from jax.sharding import Mesh, PartitionSpec as P

K2 = 256
K3 = 32
K4 = 8
LANES = 128
F32 = jnp.float32
BF16 = jnp.bfloat16
I32 = jnp.int32


def dot(a, b, precision=None):
    return lax.dot_general(
        a, b, (((1,), (0,)), ((), ())), precision=precision, preferred_element_type=F32
    )


def iota(shape, axis):
    return lax.broadcasted_iota(I32, shape, axis)


def whole(shape):
    return pl.BlockSpec(shape, lambda i, pos: (0,) * len(shape))


def call(body, pos, args, in_specs, out_shapes, flops=0, limit=32):
    single = not isinstance(out_shapes, (list, tuple))
    shapes = [out_shapes] if single else list(out_shapes)
    moved = sum(a.size * a.dtype.itemsize for a in args) + sum(
        s.size * s.dtype.itemsize for s in shapes
    )
    out = pl.pallas_call(
        body,
        grid_spec=pltpu.PrefetchScalarGridSpec(
            num_scalar_prefetch=1,
            grid=(1,),
            in_specs=in_specs,
            out_specs=[whole(s.shape) for s in shapes],
        ),
        out_shape=shapes,
        compiler_params=pltpu.CompilerParams(vmem_limit_bytes=limit * 2**20),
        cost_estimate=pl.CostEstimate(flops=flops, bytes_accessed=moved, transcendentals=0),
    )(pos, *args)
    return out[0] if single else out


def prep_kernel(pos, live, assign, parent, points, pack, give):
    groups, cap = assign.shape
    lane = iota((1, cap), 1)
    above = parent[...] * 256
    rows = [
        jnp.where(lane < live[0, b], assign[b : b + 1, :] + 1, 0) + above for b in range(groups)
    ]
    row = jnp.concatenate(rows, axis=0)
    for d in range(groups):
        pack[d] = row
    give[...] = points[...]


def replicated_count(hits):
    return dot(hits.astype(BF16), jnp.ones((hits.shape[1], LANES), BF16))


def hits_of(known, block, kdev):
    ks = iota((kdev, LANES), 0) + 1
    total = jnp.zeros((kdev, LANES), F32)
    for s in range(known.shape[0]):
        ids = known[s, pl.ds(block, 1), :] & 255
        total = total + jnp.where(ids == ks, 1.0, 0.0)
    return total


def main_kernel(pos, known, mine, theirs, out, child):
    groups, kdev = known.shape[0], known.shape[2]
    nx, cols = out.shape[0], out.shape[2]
    x, c = pos[0], pos[1]
    ks = iota((kdev, LANES), 0) + 1
    k2s = iota((K2, kdev), 0)
    total = jnp.zeros((K2, nx * cols), F32)
    children = jnp.zeros((K2, kdev), F32)
    for pair in range(groups // 2):
        lefts, parts = [], ([], [], [])
        for b in (2 * pair, 2 * pair + 1):
            inverse = 1.0 / replicated_count(hits_of(known, b, kdev))
            ids = [known[2 * x + core, b : b + 1, :] & 255 for core in (c, 1 - c)]
            onehot = jnp.concatenate(
                [jnp.where(v == ks, 1.0, 0.0).astype(BF16) for v in ids], axis=1
            )
            rows = slice(b * kdev, (b + 1) * kdev)
            sums = dot(onehot, jnp.concatenate([mine[rows, :], theirs[rows, :]], axis=0))
            sums = sums * jnp.concatenate([inverse] * nx, axis=1)
            hi = sums.astype(BF16)
            rest = sums - hi.astype(F32)
            mid = rest.astype(BF16)
            low = (rest - mid.astype(F32)).astype(BF16)
            for store, part in zip(parts, (hi, mid, low)):
                store.append(part)
            left = jnp.where((known[b, 0:1, :] >> 8) == k2s, 1.0, 0.0)
            children = children + left
            lefts.append(left.astype(BF16))
        left = jnp.concatenate(lefts, axis=1)
        for part in parts:
            total = total + dot(left, jnp.concatenate(part, axis=0))
    for j in range(nx):
        out[j] = total[:, j * cols : (j + 1) * cols]
    counts = replicated_count(children)
    ny = child.shape[0]
    rows = K2 // ny
    diagonal = iota((rows, LANES), 0) == iota((rows, LANES), 1)
    for j in range(ny):
        row = jnp.sum(
            jnp.where(diagonal, counts[j * rows : (j + 1) * rows], 0.0), axis=0, keepdims=True
        )
        child[j] = jnp.broadcast_to(row, (8, LANES))


def x_sum_kernel(pos, parts, child, out):
    ny = out.shape[0]
    rows = out.shape[1] - 8
    for j in range(ny):
        part = slice(j * rows, (j + 1) * rows)
        total = parts[0, part, :]
        for s in range(1, parts.shape[0]):
            total = total + parts[s, part, :]
        out[j, :rows] = total
        out[j, rows:] = child[j]


def y_sum_kernel(pos, parts, out):
    total = parts[0]
    for s in range(1, parts.shape[0]):
        total = total + parts[s]
    for s in range(out.shape[0]):
        out[s] = total


def z_sum_kernel(pos, parts, out):
    total = parts[0]
    for s in range(1, parts.shape[0]):
        total = total + parts[s]
    rows = out.shape[1]
    diagonal = iota((rows, LANES), 0) == iota((rows, LANES), 1)
    count = jnp.sum(
        jnp.where(diagonal, total[rows : rows + 1, :], 0.0), axis=1, keepdims=True
    )
    mean = total[:rows] / count
    for s in range(out.shape[0]):
        out[s] = mean


def mean_of(rows, parents, number):
    onehot = jnp.where(parents == iota((number, parents.shape[1]), 0), 1.0, 0.0)
    sums = dot(onehot, rows, lax.Precision.HIGHEST)
    return sums / jnp.sum(onehot, axis=1, keepdims=True)


def upper_kernel(pos, two, parent_three, parent_four, out):
    three = mean_of(two[...], parent_three[...], K3)
    four = mean_of(three, parent_four[...], K4)
    for s in range(out.shape[0]):
        out[s, :K2] = two[...]
        out[s, K2 : K2 + K3] = three
        out[s, K2 + K3 :] = four


def final_kernel(pos, kept, got, two, three, four):
    nx, cols = kept.shape[0], kept.shape[2]
    for part, core in ((kept, pos[1]), (got, 1 - pos[1])):
        for j in range(nx):
            at = pl.ds(pl.multiple_of((core * nx + j) * cols, cols), cols)
            two[:, at] = part[j, :K2]
            three[:, at] = part[j, K2 : K2 + K3]
            four[:, at] = part[j, K2 + K3 :]


def send_kernel(pos, a, b, c, after, to_a, to_b, to_c):
    to_a[...] = a[0]
    to_b[...] = b[0]
    to_c[...] = c[0]


def one_kernel(pos, known, own, *refs):
    arrived, (keep, give) = refs[:-2], refs[-2:]
    x, c = pos[0], pos[1]
    kdev = keep.shape[0]
    nx = len(arrived) + 1
    ks = iota((kdev, LANES), 0) + 1
    for out, core in ((keep, c), (give, 1 - c)):
        at = pl.ds(pl.multiple_of(core * kdev, kdev), kdev)
        onehots, rows = [], []
        for k in range(nx):
            source = lax.rem(x + nx - k, nx)
            ids = known[2 * source + c, pl.ds(2 * x + core, 1), :] & 255
            onehots.append(jnp.where(ids == ks, 1.0, 0.0).astype(BF16))
            rows.append(own[0, at, :] if k == 0 else arrived[k - 1][at, :])
        out[...] = dot(jnp.concatenate(onehots, axis=1), jnp.concatenate(rows, axis=0))


def one_mean_kernel(pos, known, keep, got, out):
    kdev = keep.shape[0]
    count = replicated_count(hits_of(known, 2 * pos[0] + pos[1], kdev))
    for j in range(out.shape[1] // LANES):
        at = slice(j * LANES, (j + 1) * LANES)
        out[:, at] = (keep[:, at] + got[:, at]) / count


def exchange(rows, axes):
    return lax.all_to_all(rows, axes, split_axis=0, concat_axis=0, tiled=True)


def swap(rows):
    return lax.ppermute(rows, "c", [(0, 1), (1, 0)])


def local(points, send_counts, assign_one, parent_two, parent_three, parent_four):
    nx, nc, ny, nz = (lax.axis_size(a) for a in ("x", "c", "y", "z"))
    groups = nx * nc
    slots, depth = points.shape
    cap = slots // groups
    kdev = parent_two.shape[0]
    half = depth // nc
    cols = half // nx
    rows = K2 // ny
    pos = jnp.stack([lax.axis_index("x"), lax.axis_index("c")]).astype(I32)
    shape = jax.ShapeDtypeStruct

    pack, give = call(
        prep_kernel,
        pos,
        (send_counts, assign_one.reshape(groups, cap), parent_two.reshape(1, kdev), points),
        [
            pl.BlockSpec(memory_space=pltpu.SMEM),
            whole((groups, cap)),
            whole((1, kdev)),
            pl.BlockSpec((slots, half), lambda i, pos: (0, 1 - pos[1])),
        ],
        (shape((groups, groups, cap), I32), shape((slots, half), BF16)),
    )
    known = exchange(pack, ("x", "c"))
    theirs = swap(give)

    partial, child = call(
        main_kernel,
        pos,
        (known, points, theirs),
        [
            whole((groups, groups, cap)),
            pl.BlockSpec((slots, half), lambda i, pos: (0, pos[1])),
            whole((slots, half)),
        ],
        (shape((nx, K2, cols), F32), shape((ny, 8, LANES), F32)),
        flops=2 * (2 * slots * kdev * half + 3 * K2 * slots * half),
    )
    partial = exchange(partial, "x")
    sums = call(
        x_sum_kernel,
        pos,
        (partial, child),
        [whole((nx, K2, cols)), whole((ny, 8, LANES))],
        shape((ny, rows + 8, cols), F32),
    )
    byx = points.reshape(nx, nc * cap, depth)
    sent = call(
        send_kernel,
        pos,
        (byx, byx, byx, sums),
        [
            pl.BlockSpec((1, nc * cap, depth), lambda i, pos, k=k: (lax.rem(pos[0] + k, nx), 0, 0))
            for k in range(1, nx)
        ]
        + [pl.BlockSpec(memory_space=pl.ANY)],
        [shape((nc * cap, depth), BF16)] * (nx - 1),
    )
    arrived = [
        lax.ppermute(v, "x", [(j, (j + k) % nx) for j in range(nx)])
        for k, v in zip(range(1, nx), sent)
    ]

    sums = exchange(sums, "y")
    sums = call(
        y_sum_kernel,
        pos,
        (sums,),
        [whole((ny, rows + 8, cols))],
        shape((nz, rows + 8, cols), F32),
    )
    sums = exchange(sums, "z")
    two = call(
        z_sum_kernel, pos, (sums,), [whole((nz, rows + 8, cols))], shape((ny, rows, cols), F32)
    )
    two = exchange(two, "y").reshape(K2, cols)
    height = K2 + K3 + K4
    upper = call(
        upper_kernel,
        pos,
        (two, parent_three.reshape(1, K2), parent_four.reshape(1, K3)),
        [whole((K2, cols)), whole((1, K2)), whole((1, K3))],
        shape((nx, height, cols), F32),
    )
    upper = exchange(upper, "x")
    other = swap(upper)
    two, three, four = call(
        final_kernel,
        pos,
        (upper, other),
        [whole((nx, height, cols))] * 2,
        (shape((K2, depth), F32), shape((K3, depth), F32), shape((K4, depth), F32)),
    )

    keep, give = call(
        one_kernel,
        pos,
        (known, byx, *arrived),
        [
            whole((groups, groups, cap)),
            pl.BlockSpec((1, nc * cap, depth), lambda i, pos: (pos[0], 0, 0)),
        ]
        + [whole((nc * cap, depth))] * (nx - 1),
        (shape((kdev, depth), F32), shape((kdev, depth), F32)),
        flops=2 * slots * kdev * depth,
    )
    one = call(
        one_mean_kernel,
        pos,
        (known, keep, swap(give)),
        [whole((groups, groups, cap)), whole((kdev, depth)), whole((kdev, depth))],
        shape((kdev, depth), F32),
    )
    return one, two, three, four


def solution(mesh):
    npts, groups = mesh.devices.shape
    ny = min(8, npts)
    fine = Mesh(mesh.devices.reshape(ny, npts // ny, groups // 2, 2), ("y", "z", "x", "c"))
    every = ("y", "z", "x", "c")
    placed = (P(every, None), P(every, None), P(every), P(every), P(), P())
    return jax.shard_map(
        local,
        mesh=fine,
        in_specs=placed,
        out_specs=(P(every, None), P(), P(), P()),
        check_vma=False,
    )
```

```python
import functools

import jax
import jax.numpy as jnp
from jax import lax
from jax.experimental import pallas as pl
from jax.experimental.pallas import tpu as pltpu
from jax.sharding import Mesh, PartitionSpec as P

K2 = 256
K3 = 32
K4 = 8
LANES = 128
F32 = jnp.float32
BF16 = jnp.bfloat16
I32 = jnp.int32


def dot(a, b, precision=None):
    return lax.dot_general(
        a, b, (((1,), (0,)), ((), ())), precision=precision, preferred_element_type=F32
    )


def iota(shape, axis):
    return lax.broadcasted_iota(I32, shape, axis)


def whole(shape):
    return pl.BlockSpec(shape, lambda i, pos: (0,) * len(shape))


def call(body, pos, args, in_specs, out_shapes, flops=0, limit=24, scratch=(), far=0):
    single = not isinstance(out_shapes, (list, tuple))
    shapes = [out_shapes] if single else list(out_shapes)
    moved = sum(a.size * a.dtype.itemsize for a in args) + sum(
        s.size * s.dtype.itemsize for s in shapes
    )
    out = pl.pallas_call(
        body,
        grid_spec=pltpu.PrefetchScalarGridSpec(
            num_scalar_prefetch=1,
            grid=(1,),
            in_specs=in_specs,
            out_specs=[whole(s.shape) for s in shapes[: len(shapes) - far]]
            + [pl.BlockSpec(memory_space=pltpu.HBM)] * far,
            scratch_shapes=scratch,
        ),
        out_shape=shapes,
        compiler_params=pltpu.CompilerParams(vmem_limit_bytes=limit * 2**20),
        cost_estimate=pl.CostEstimate(flops=flops, bytes_accessed=moved, transcendentals=0),
    )(pos, *args)
    return out[0] if single else out


def prep_kernel(live, assign, parent, pack, live_s, assign_v, parent_v, sems):
    groups, cap = assign.shape
    copies = [
        pltpu.make_async_copy(source, target, sems.at[i])
        for i, (source, target) in enumerate(
            [(live, live_s), (assign, assign_v), (parent, parent_v)]
        )
    ]
    for copy in copies:
        copy.start()
    for copy in copies:
        copy.wait()
    lane = iota((1, cap), 1)
    above = parent_v[...] * 256
    rows = [
        jnp.where(lane < live_s[0, b], assign_v[b : b + 1, :] + 1, 0) + above
        for b in range(groups)
    ]
    row = jnp.concatenate(rows, axis=0)
    for d in range(groups):
        pack[d] = row


def replicated_count(hits):
    return dot(hits.astype(BF16), jnp.ones((hits.shape[1], LANES), BF16))


def hits_of(known, block, kdev):
    ks = iota((kdev, LANES), 0) + 1
    total = jnp.zeros((kdev, LANES), F32)
    for s in range(known.shape[0]):
        ids = known[s, pl.ds(block, 1), :] & 255
        total = total + jnp.where(ids == ks, 1.0, 0.0)
    return total


def main_kernel(pos, known, mine, theirs, out, child, *refs):
    sent, (weights, sems) = refs[:-2], refs[-2:]
    groups, kdev = known.shape[0], known.shape[2]
    nx, height, lanes = out.shape
    half = weights.shape[1] // 3
    x, c = pos[0], pos[1]
    copies = []
    for k, target in enumerate(sent):
        block = 2 * lax.rem(x + k, nx) + c
        at = pl.ds(pl.multiple_of(block * kdev, kdev), kdev)
        for which, rows in enumerate((mine, theirs)):
            copies.append(
                pltpu.make_async_copy(rows.at[at, :], target.at[which], sems.at[k, which])
            )
    for copy in copies:
        copy.start()
    ks = iota((kdev, LANES), 0) + 1
    k2s = iota((half, kdev), 0) + c * half
    diagonal = iota((kdev, LANES), 0) == iota((kdev, LANES), 1)
    children = jnp.zeros((half, kdev), F32)
    for b in range(groups):
        inverse = 1.0 / replicated_count(hits_of(known, b, kdev))
        inverse = jnp.sum(jnp.where(diagonal, inverse, 0.0), axis=0, keepdims=True)
        chosen = (known[b, 0:1, :] >> 8) == k2s
        children = children + jnp.where(chosen, 1.0, 0.0)
        weight = jnp.where(chosen, inverse, 0.0)
        hi = weight.astype(BF16)
        rest = weight - hi.astype(F32)
        mid = rest.astype(BF16)
        low = (rest - mid.astype(F32)).astype(BF16)
        parts = jnp.concatenate([hi, mid, low], axis=0)
        for which, core in ((0, c), (1, 1 - c)):
            ids = known[2 * x + core, b : b + 1, :] & 255
            onehot = jnp.where(ids == ks, 1.0, 0.0).astype(BF16)
            weights[which, :, b * kdev : (b + 1) * kdev] = dot(parts, onehot).astype(BF16)
    for j in range(nx):
        at = slice(j * 2 * lanes, (j + 1) * 2 * lanes)
        total = dot(weights[0], mine[:, at]) + dot(weights[1], theirs[:, at])
        total = total[:half] + total[half : 2 * half] + total[2 * half :]
        out[j, :half] = total[:, :lanes]
        out[j, half:] = total[:, lanes:]
    counts = replicated_count(children)
    ny = child.shape[0]
    rows = half // ny
    diagonal = iota((rows, LANES), 0) == iota((rows, LANES), 1)
    for j in range(ny):
        row = jnp.sum(
            jnp.where(diagonal, counts[j * rows : (j + 1) * rows], 0.0), axis=0, keepdims=True
        )
        child[j] = jnp.broadcast_to(row, (8, LANES))
    for copy in copies:
        copy.wait()


def x_sum_kernel(pos, parts, child, out):
    ny = out.shape[0]
    rows = (out.shape[1] - 8) // 2
    half = parts.shape[1] // 2
    for j in range(ny):
        for h in range(2):
            part = slice(h * half + j * rows, h * half + (j + 1) * rows)
            total = parts[0, part, :]
            for s in range(1, parts.shape[0]):
                total = total + parts[s, part, :]
            out[j, h * rows : (h + 1) * rows] = total
        out[j, 2 * rows :] = child[j]


def y_sum_kernel(pos, parts, out):
    total = parts[0]
    for s in range(1, parts.shape[0]):
        total = total + parts[s]
    for s in range(out.shape[0]):
        out[s] = total


def z_sum_kernel(pos, parts, out):
    total = parts[0]
    for s in range(1, parts.shape[0]):
        total = total + parts[s]
    rows = out.shape[1] // 2
    diagonal = iota((rows, LANES), 0) == iota((rows, LANES), 1)
    count = jnp.sum(
        jnp.where(diagonal, total[2 * rows : 2 * rows + 1, :], 0.0), axis=1, keepdims=True
    )
    for h in range(2):
        mean = total[h * rows : (h + 1) * rows] / count
        for s in range(out.shape[0]):
            out[s, h * rows : (h + 1) * rows] = mean


def mean_of(rows, parents, number):
    onehot = jnp.where(parents == iota((number, parents.shape[1]), 0), 1.0, 0.0)
    sums = dot(onehot, rows, lax.Precision.HIGHEST)
    return sums / jnp.sum(onehot, axis=1, keepdims=True)


def wide_kernel(pos, two, *refs):
    out = refs[-1]
    ny = two.shape[0]
    rows = two.shape[1] // 2
    half = out.shape[1] // 2
    for h in range(2):
        for j in range(ny):
            part = two[j, h * rows : (h + 1) * rows]
            for s in range(out.shape[0]):
                out[s, h * half + j * rows : h * half + (j + 1) * rows] = part


def final_kernel(pos, kept, got, parent_three, parent_four, two, three, four):
    nx, lanes = kept.shape[0], kept.shape[2]
    half = kept.shape[1] // 2
    for part, core in ((kept, pos[1]), (got, 1 - pos[1])):
        to = pl.ds(pl.multiple_of(core * half, half), half)
        for j in range(nx):
            for h in range(2):
                at = slice((2 * j + h) * lanes, (2 * j + h + 1) * lanes)
                two[to, at] = part[j, h * half : (h + 1) * half]
    mean = mean_of(two[...], parent_three[...], K3)
    three[...] = mean
    four[...] = mean_of(mean, parent_four[...], K4)


def one_kernel(pos, known, *refs):
    arrived, out = refs[:-1], refs[-1]
    x, c = pos[0], pos[1]
    kdev = out.shape[0]
    nx = len(arrived)
    ks = iota((kdev, LANES), 0) + 1
    onehots, rows = [], []
    for k in range(nx):
        source = lax.rem(x + nx - k, nx)
        for which, core in ((0, c), (1, 1 - c)):
            ids = known[2 * source + core, pl.ds(2 * x + c, 1), :] & 255
            onehots.append(jnp.where(ids == ks, 1.0, 0.0).astype(BF16))
            rows.append(arrived[k][which])
    sums = dot(jnp.concatenate(onehots, axis=1), jnp.concatenate(rows, axis=0))
    count = replicated_count(hits_of(known, 2 * x + c, kdev))
    for j in range(out.shape[1] // LANES):
        at = slice(j * LANES, (j + 1) * LANES)
        out[:, at] = sums[:, at] / count


def exchange(rows, axes):
    return lax.all_to_all(rows, axes, split_axis=0, concat_axis=0, tiled=True)


def swap(rows):
    return lax.ppermute(rows, "c", [(0, 1), (1, 0)])


def local(points, send_counts, assign_one, parent_two, parent_three, parent_four):
    nx, nc, ny, nz = (lax.axis_size(a) for a in ("x", "c", "y", "z"))
    groups = nx * nc
    slots, depth = points.shape
    cap = slots // groups
    kdev = parent_two.shape[0]
    half = K2 // nc
    rows = half // ny
    assert depth == 2 * nx * LANES and nc == 2 and cap == kdev == LANES
    pos = jnp.stack([lax.axis_index("x"), lax.axis_index("c")]).astype(I32)
    shape = jax.ShapeDtypeStruct

    pack = pl.pallas_call(
        prep_kernel,
        in_specs=[pl.BlockSpec(memory_space=pltpu.HBM)] * 3,
        out_specs=pl.BlockSpec(memory_space=pltpu.VMEM),
        out_shape=shape((groups, groups, cap), I32),
        scratch_shapes=[
            pltpu.SMEM((1, groups), I32),
            pltpu.VMEM((groups, cap), I32),
            pltpu.VMEM((1, kdev), I32),
            pltpu.SemaphoreType.DMA((3,)),
        ],
        compiler_params=pltpu.CompilerParams(vmem_limit_bytes=63 * 2**20),
    )(send_counts, assign_one.reshape(groups, cap), parent_two.reshape(1, kdev))
    known = exchange(pack, ("x", "c"))
    theirs = swap(points)

    partial, child, *sent = call(
        main_kernel,
        pos,
        (known, points, theirs),
        [whole((groups, groups, cap)), whole((slots, depth)), whole((slots, depth))],
        [shape((nx, 2 * half, LANES), F32), shape((ny, 8, LANES), F32)]
        + [shape((nc, cap, depth), BF16)] * nx,
        flops=2 * 6 * slots * half * depth,
        scratch=[
            pltpu.VMEM((nc, 3 * half, slots), BF16),
            pltpu.SemaphoreType.DMA((nx, nc)),
        ],
        far=nx,
    )
    partial = exchange(partial, "x")

    sums = call(
        x_sum_kernel,
        pos,
        (partial, child),
        [whole((nx, 2 * half, LANES)), whole((ny, 8, LANES))],
        shape((ny, 2 * rows + 8, LANES), F32),
    )
    arrived = [
        lax.ppermute(v, "x", [(j, (j + k) % nx) for j in range(nx)])
        for k, v in enumerate(sent)
        if k > 0
    ]

    sums = exchange(sums, "y")
    sums = call(
        y_sum_kernel,
        pos,
        (sums,),
        [whole((ny, 2 * rows + 8, LANES))],
        shape((nz, 2 * rows + 8, LANES), F32),
    )
    sums = exchange(sums, "z")
    two = call(
        z_sum_kernel, pos, (sums,), [whole((nz, 2 * rows + 8, LANES))], shape((ny, 2 * rows, LANES), F32)
    )
    two = exchange(two, "y")
    two = call(
        wide_kernel,
        pos,
        (two, *arrived),
        [whole((ny, 2 * rows, LANES))] + [pl.BlockSpec(memory_space=pl.ANY)] * len(arrived),
        shape((nx, 2 * half, LANES), F32),
    )
    two = exchange(two, "x")
    two, three, four = call(
        final_kernel,
        pos,
        (two, swap(two), parent_three.reshape(1, K2), parent_four.reshape(1, K3)),
        [whole((nx, 2 * half, LANES))] * 2 + [whole((1, K2)), whole((1, K3))],
        [shape((n, depth), F32) for n in (K2, K3, K4)],
    )
    one = call(
        one_kernel,
        pos,
        (known, sent[0], *arrived),
        [whole((groups, groups, cap))] + [whole((nc, cap, depth))] * nx,
        shape((kdev, depth), F32),
        flops=2 * slots * kdev * depth,
    )
    return one, two, three, four


def solution(mesh):
    npts, groups = mesh.devices.shape
    ny = min(8, npts)
    fine = Mesh(mesh.devices.reshape(ny, npts // ny, groups // 2, 2), ("y", "z", "x", "c"))
    every = ("y", "z", "x", "c")
    placed = (P(every, None), P(every, None), P(every), P(every), P(), P())
    return jax.shard_map(
        local,
        mesh=fine,
        in_specs=placed,
        out_specs=(P(every, None), P(), P(), P()),
        check_vma=False,
    )
```

```python
import functools

import jax
import jax.numpy as jnp
from jax import lax
from jax.experimental import pallas as pl
from jax.experimental.pallas import tpu as pltpu
from jax.sharding import Mesh, PartitionSpec as P

K2 = 256
K3 = 32
K4 = 8
LANES = 128
F32 = jnp.float32
BF16 = jnp.bfloat16
I32 = jnp.int32


def dot(a, b, precision=None):
    return lax.dot_general(
        a, b, (((1,), (0,)), ((), ())), precision=precision, preferred_element_type=F32
    )


def iota(shape, axis):
    return lax.broadcasted_iota(I32, shape, axis)


def whole(shape):
    return pl.BlockSpec(shape, lambda i, pos: (0,) * len(shape))


def call(body, pos, args, in_specs, out_shapes, flops=0, limit=24, scratch=(), far=0):
    single = not isinstance(out_shapes, (list, tuple))
    shapes = [out_shapes] if single else list(out_shapes)
    moved = sum(a.size * a.dtype.itemsize for a in args) + sum(
        s.size * s.dtype.itemsize for s in shapes
    )
    out = pl.pallas_call(
        body,
        grid_spec=pltpu.PrefetchScalarGridSpec(
            num_scalar_prefetch=1,
            grid=(1,),
            in_specs=in_specs,
            out_specs=[whole(s.shape) for s in shapes[: len(shapes) - far]]
            + [pl.BlockSpec(memory_space=pltpu.HBM)] * far,
            scratch_shapes=scratch,
        ),
        out_shape=shapes,
        compiler_params=pltpu.CompilerParams(vmem_limit_bytes=limit * 2**20),
        cost_estimate=pl.CostEstimate(flops=flops, bytes_accessed=moved, transcendentals=0),
    )(pos, *args)
    return out[0] if single else out


def prep_kernel(live, assign, parent, pack, live_s, assign_v, parent_v, sems):
    groups, cap = assign.shape
    copies = [
        pltpu.make_async_copy(source, target, sems.at[i])
        for i, (source, target) in enumerate(
            [(live, live_s), (assign, assign_v), (parent, parent_v)]
        )
    ]
    for copy in copies:
        copy.start()
    for copy in copies:
        copy.wait()
    lane = iota((1, cap), 1)
    above = parent_v[...] * 256
    rows = [
        jnp.where(lane < live_s[0, b], assign_v[b : b + 1, :] + 1, 0) + above
        for b in range(groups)
    ]
    row = jnp.concatenate(rows, axis=0)
    for d in range(groups):
        pack[d] = row


def replicated_count(hits):
    return dot(hits.astype(BF16), jnp.ones((hits.shape[1], LANES), BF16))


def hits_of(known, block, kdev):
    ks = iota((kdev, LANES), 0) + 1
    total = jnp.zeros((kdev, LANES), F32)
    for s in range(known.shape[0]):
        ids = known[s, pl.ds(block, 1), :] & 255
        total = total + jnp.where(ids == ks, 1.0, 0.0)
    return total


def main_kernel(pos, known, mine_far, theirs_far, out, child, *refs):
    sent, (weights, mine, theirs, loads, sems) = refs[:-5], refs[-5:]
    fetches = [
        pltpu.make_async_copy(source, target, loads.at[i])
        for i, (source, target) in enumerate([(mine_far, mine), (theirs_far, theirs)])
    ]
    for fetch in fetches:
        fetch.start()
    groups, kdev = known.shape[0], known.shape[2]
    nx, height, lanes = out.shape
    half = weights.shape[1] // 3
    x, c = pos[0], pos[1]
    copies = []
    for k, target in enumerate(sent):
        block = 2 * lax.rem(x + k, nx) + c
        at = pl.ds(pl.multiple_of(block * kdev, kdev), kdev)
        for which, rows in enumerate((mine, theirs)):
            copies.append(
                pltpu.make_async_copy(rows.at[at, :], target.at[which], sems.at[k, which])
            )
    ks = iota((kdev, LANES), 0) + 1
    k2s = iota((half, kdev), 0) + c * half
    diagonal = iota((kdev, LANES), 0) == iota((kdev, LANES), 1)
    children = jnp.zeros((half, kdev), F32)
    for b in range(groups):
        inverse = 1.0 / replicated_count(hits_of(known, b, kdev))
        inverse = jnp.sum(jnp.where(diagonal, inverse, 0.0), axis=0, keepdims=True)
        chosen = (known[b, 0:1, :] >> 8) == k2s
        children = children + jnp.where(chosen, 1.0, 0.0)
        weight = jnp.where(chosen, inverse, 0.0)
        hi = weight.astype(BF16)
        rest = weight - hi.astype(F32)
        mid = rest.astype(BF16)
        low = (rest - mid.astype(F32)).astype(BF16)
        parts = jnp.concatenate([hi, mid, low], axis=0)
        for which, core in ((0, c), (1, 1 - c)):
            ids = known[2 * x + core, b : b + 1, :] & 255
            onehot = jnp.where(ids == ks, 1.0, 0.0).astype(BF16)
            weights[which, :, b * kdev : (b + 1) * kdev] = dot(parts, onehot).astype(BF16)
    for which, rows in enumerate((mine, theirs)):
        fetches[which].wait()
        for copy in copies[which::2]:
            copy.start()
        for j in range(nx):
            at = slice(j * 2 * lanes, (j + 1) * 2 * lanes)
            total = dot(weights[which], rows[:, at])
            total = total[:half] + total[half : 2 * half] + total[2 * half :]
            if which == 0:
                out[j, :half] = total[:, :lanes]
                out[j, half:] = total[:, lanes:]
            else:
                out[j, :half] = out[j, :half] + total[:, :lanes]
                out[j, half:] = out[j, half:] + total[:, lanes:]
    counts = replicated_count(children)
    ny = child.shape[0]
    rows = half // ny
    diagonal = iota((rows, LANES), 0) == iota((rows, LANES), 1)
    for j in range(ny):
        row = jnp.sum(
            jnp.where(diagonal, counts[j * rows : (j + 1) * rows], 0.0), axis=0, keepdims=True
        )
        child[j] = jnp.broadcast_to(row, (8, LANES))
    for copy in copies:
        copy.wait()


def x_sum_kernel(pos, parts, child, out):
    ny = out.shape[0]
    rows = (out.shape[1] - 8) // 2
    half = parts.shape[1] // 2
    for j in range(ny):
        for h in range(2):
            part = slice(h * half + j * rows, h * half + (j + 1) * rows)
            total = parts[0, part, :]
            for s in range(1, parts.shape[0]):
                total = total + parts[s, part, :]
            out[j, h * rows : (h + 1) * rows] = total
        out[j, 2 * rows :] = child[j]


def y_sum_kernel(pos, parts, out):
    total = parts[0]
    for s in range(1, parts.shape[0]):
        total = total + parts[s]
    for s in range(out.shape[0]):
        out[s] = total


def z_sum_kernel(pos, parts, out):
    total = parts[0]
    for s in range(1, parts.shape[0]):
        total = total + parts[s]
    rows = out.shape[1] // 2
    diagonal = iota((rows, LANES), 0) == iota((rows, LANES), 1)
    count = jnp.sum(
        jnp.where(diagonal, total[2 * rows : 2 * rows + 1, :], 0.0), axis=1, keepdims=True
    )
    for h in range(2):
        mean = total[h * rows : (h + 1) * rows] / count
        for s in range(out.shape[0]):
            out[s, h * rows : (h + 1) * rows] = mean


def mean_of(rows, parents, number):
    onehot = jnp.where(parents == iota((number, parents.shape[1]), 0), 1.0, 0.0)
    sums = dot(onehot, rows, lax.Precision.HIGHEST)
    return sums / jnp.sum(onehot, axis=1, keepdims=True)


def wide_kernel(pos, two, *refs):
    out = refs[-1]
    ny = two.shape[0]
    rows = two.shape[1] // 2
    half = out.shape[1] // 2
    for h in range(2):
        for j in range(ny):
            part = two[j, h * rows : (h + 1) * rows]
            for s in range(out.shape[0]):
                out[s, h * half + j * rows : h * half + (j + 1) * rows] = part


def final_kernel(pos, kept, got, parent_three, parent_four, two, three, four):
    nx, lanes = kept.shape[0], kept.shape[2]
    half = kept.shape[1] // 2
    for part, core in ((kept, pos[1]), (got, 1 - pos[1])):
        to = pl.ds(pl.multiple_of(core * half, half), half)
        for j in range(nx):
            for h in range(2):
                at = slice((2 * j + h) * lanes, (2 * j + h + 1) * lanes)
                two[to, at] = part[j, h * half : (h + 1) * half]
    mean = mean_of(two[...], parent_three[...], K3)
    three[...] = mean
    four[...] = mean_of(mean, parent_four[...], K4)


def one_kernel(pos, known, *refs):
    arrived, out = refs[:-1], refs[-1]
    x, c = pos[0], pos[1]
    kdev = out.shape[0]
    nx = len(arrived)
    ks = iota((kdev, LANES), 0) + 1
    onehots, rows = [], []
    for k in range(nx):
        source = lax.rem(x + nx - k, nx)
        for which, core in ((0, c), (1, 1 - c)):
            ids = known[2 * source + core, pl.ds(2 * x + c, 1), :] & 255
            onehots.append(jnp.where(ids == ks, 1.0, 0.0).astype(BF16))
            rows.append(arrived[k][which])
    sums = dot(jnp.concatenate(onehots, axis=1), jnp.concatenate(rows, axis=0))
    count = replicated_count(hits_of(known, 2 * x + c, kdev))
    for j in range(out.shape[1] // LANES):
        at = slice(j * LANES, (j + 1) * LANES)
        out[:, at] = sums[:, at] / count


def exchange(rows, axes):
    return lax.all_to_all(rows, axes, split_axis=0, concat_axis=0, tiled=True)


def swap(rows):
    return lax.ppermute(rows, "c", [(0, 1), (1, 0)])


def local(points, send_counts, assign_one, parent_two, parent_three, parent_four):
    nx, nc, ny, nz = (lax.axis_size(a) for a in ("x", "c", "y", "z"))
    groups = nx * nc
    slots, depth = points.shape
    cap = slots // groups
    kdev = parent_two.shape[0]
    half = K2 // nc
    rows = half // ny
    assert depth == 2 * nx * LANES and nc == 2 and cap == kdev == LANES
    pos = jnp.stack([lax.axis_index("x"), lax.axis_index("c")]).astype(I32)
    shape = jax.ShapeDtypeStruct

    pack = pl.pallas_call(
        prep_kernel,
        in_specs=[pl.BlockSpec(memory_space=pltpu.HBM)] * 3,
        out_specs=pl.BlockSpec(memory_space=pltpu.VMEM),
        out_shape=shape((groups, groups, cap), I32),
        scratch_shapes=[
            pltpu.SMEM((1, groups), I32),
            pltpu.VMEM((groups, cap), I32),
            pltpu.VMEM((1, kdev), I32),
            pltpu.SemaphoreType.DMA((3,)),
        ],
        compiler_params=pltpu.CompilerParams(vmem_limit_bytes=63 * 2**20),
    )(send_counts, assign_one.reshape(groups, cap), parent_two.reshape(1, kdev))
    known = exchange(pack, ("x", "c"))
    theirs = swap(points)

    partial, child, *sent = call(
        main_kernel,
        pos,
        (known, points, theirs),
        [whole((groups, groups, cap))] + [pl.BlockSpec(memory_space=pltpu.HBM)] * 2,
        [shape((nx, 2 * half, LANES), F32), shape((ny, 8, LANES), F32)]
        + [shape((nc, cap, depth), BF16)] * nx,
        flops=2 * 6 * slots * half * depth,
        scratch=[
            pltpu.VMEM((nc, 3 * half, slots), BF16),
            pltpu.VMEM((slots, depth), BF16),
            pltpu.VMEM((slots, depth), BF16),
            pltpu.SemaphoreType.DMA((2,)),
            pltpu.SemaphoreType.DMA((nx, nc)),
        ],
        far=nx,
        limit=24,
    )
    partial = exchange(partial, "x")

    sums = call(
        x_sum_kernel,
        pos,
        (partial, child),
        [whole((nx, 2 * half, LANES)), whole((ny, 8, LANES))],
        shape((ny, 2 * rows + 8, LANES), F32),
    )
    arrived = [
        lax.ppermute(v, "x", [(j, (j + k) % nx) for j in range(nx)])
        for k, v in enumerate(sent)
        if k > 0
    ]

    sums = exchange(sums, "y")
    sums = call(
        y_sum_kernel,
        pos,
        (sums,),
        [whole((ny, 2 * rows + 8, LANES))],
        shape((nz, 2 * rows + 8, LANES), F32),
    )
    sums = exchange(sums, "z")
    two = call(
        z_sum_kernel, pos, (sums,), [whole((nz, 2 * rows + 8, LANES))], shape((ny, 2 * rows, LANES), F32)
    )
    two = exchange(two, "y")
    two = call(
        wide_kernel,
        pos,
        (two, *arrived),
        [whole((ny, 2 * rows, LANES))] + [pl.BlockSpec(memory_space=pl.ANY)] * len(arrived),
        shape((nx, 2 * half, LANES), F32),
    )
    two = exchange(two, "x")
    two, three, four = call(
        final_kernel,
        pos,
        (two, swap(two), parent_three.reshape(1, K2), parent_four.reshape(1, K3)),
        [whole((nx, 2 * half, LANES))] * 2 + [whole((1, K2)), whole((1, K3))],
        [shape((n, depth), F32) for n in (K2, K3, K4)],
    )
    one = call(
        one_kernel,
        pos,
        (known, sent[0], *arrived),
        [whole((groups, groups, cap))] + [whole((nc, cap, depth))] * nx,
        shape((kdev, depth), F32),
        flops=2 * slots * kdev * depth,
    )
    return one, two, three, four


def solution(mesh):
    npts, groups = mesh.devices.shape
    ny = min(8, npts)
    fine = Mesh(mesh.devices.reshape(ny, npts // ny, groups // 2, 2), ("y", "z", "x", "c"))
    every = ("y", "z", "x", "c")
    placed = (P(every, None), P(every, None), P(every), P(every), P(), P())
    return jax.shard_map(
        local,
        mesh=fine,
        in_specs=placed,
        out_specs=(P(every, None), P(), P(), P()),
        check_vma=False,
    )
```
